256 devices in a mesh: batch: 2 (over z_lo), seq: 16 (over y, z_hi), head: 8 (over x, core).
Axes of the slice: x: 4, y: 4, z: 8 (z_hi: 4, z_lo: 2; z = z_hi * 2 + z_lo), core: 2. Of those that a mesh axis runs over, the one named last changes fastest.
Arguments:
- queries: bfloat16 [49152, 3072], P(('batch', 'seq'), 'head'), parts along dimension 0, may hold values from -120 to 120
- key_vectors: bfloat16 [49152, 3072], P(('batch', 'seq'), 'head'), parts along dimension 0, may hold values from -4 to 4
- value_vectors: bfloat16 [49152, 3072], P(('batch', 'seq'), 'head'), parts along dimension 0, may hold values from -6 to 6
- out_weight: bfloat16 [3072, 3072], P('head'), may hold values from -0.109375 to 0.109375
- window_start: int32 [128, 2], P(('batch', 'seq')), parts along dimension 0, may hold values from 0 to 13, as said below
Outputs:
- projected: bfloat16 [49152, 3072], P(('batch', 'seq', 'head')), parts along dimension 0
The draws below stay inside these ranges and needn't reach their ends.
There are 2 independent parts, one for each index of `batch`. The reference program is written for one: setup_inputs(seed, part) draws one part's arguments, and reference() takes and returns one part's arrays. A program takes and returns all parts, laid end to end along the dimension named above; an argument that names none is the same for every part. Nothing has to cross between parts.
Inputs may be any that keep to these rules, and one draw needn't show every extreme that they name: `window_start`: for tile g of temporal index a and column index c, the temporal start t satisfies a - 2 <= t <= a and t + 3 <= 16, and the column start w satisfies c - 2 <= w <= c and w + 3 <= 4.
All inputs are finite; a program needn't handle non-finite values.
Results may differ from the reference program's by a relative error of at most 0.017.
Values may be sent and summed in bfloat16 or wider, within the bound.
A program may use at most 128 MiB of HBM per device.

```python
from functools import partial
import jax
import jax.numpy as jnp
from jax import lax

HEADS = 24
DH = 128
FEATURES = 3072
TILE = 384
WT = 3
WW = 3
WTILES = 4
SLABS = 16
TOKENS = 24576
TILES = 64
HPD = 3
N_HEAD = 8


def shared_draw(key):
    base_rows = jax.random.truncated_normal(jax.random.fold_in(key, 101), -4.0, 4.0, (TOKENS, HEADS * DH), jnp.float32)
    return base_rows


def draw_key_vectors(key, part):
    base_rows = shared_draw(key)
    return base_rows.astype(jnp.bfloat16)


def draw_queries(key, part):
    key = jax.random.fold_in(key, 5)
    return jnp.clip(jax.random.normal(key, (TOKENS, HEADS * DH), jnp.float32), -6.0, 6.0).astype(jnp.bfloat16)


def draw_window_start(key, part):
    key = jax.random.fold_in(key, 9)
    tile_ids = jnp.arange(TILES, dtype=jnp.int32)
    temporal = tile_ids // WTILES
    column = tile_ids % WTILES
    back_time = jax.random.randint(jax.random.fold_in(key, 1), (TILES,), 0, WT)
    back_column = jax.random.randint(jax.random.fold_in(key, 2), (TILES,), 0, WW)
    first_time = jnp.clip(temporal - back_time, 0, SLABS - WT)
    first_column = jnp.clip(column - back_column, 0, WTILES - WW)
    return jnp.stack([first_time, first_column], axis=1).astype(jnp.int32)


def block_levels(key, dims, pieces, low, largest):
    level, own = 1.0, jax.random.fold_in(key, 6)
    for dim, parts in pieces:
        heights = jnp.exp(jax.random.uniform(jax.random.fold_in(own, dim), (parts,), jnp.float32, low / len(pieces), largest / len(pieces)))
        level = level * jnp.repeat(heights, dims[dim] // parts).reshape([-1 if axis == dim else 1 for axis in range(len(dims))])
    return level


def centred(key, shape, spread, most, shards=(), kind=jnp.bfloat16):
    factor_of = block_levels(key, shape, shards, -0.22, 0.18) if shards else 1.0
    values = jax.random.normal(key, shape, jnp.float32) * spread * factor_of
    return jnp.minimum(jnp.maximum(values, -most), most).astype(kind)


def setup_inputs(seed: int = 0, part: int = 0) -> dict:
    seeds = jax.random.split(jax.random.key(seed), 6)
    part_splits = jax.random.split(jax.random.fold_in(seeds[5], part), 6)
    queries = draw_queries(jax.random.fold_in(jax.random.fold_in(seeds[5], part), 71), part)
    key_vectors = draw_key_vectors(jax.random.fold_in(jax.random.fold_in(seeds[5], part), 71), part)
    value_vectors = centred(part_splits[2], (TOKENS, FEATURES), 1.0, 6.0, ((0, 16), (1, 8)))
    out_weight = centred(seeds[3], (FEATURES, FEATURES), FEATURES ** -0.5, 0.109375, ((0, 8),))
    window_start = draw_window_start(jax.random.fold_in(jax.random.fold_in(seeds[5], part), 71), part)
    return {"queries": queries, "key_vectors": key_vectors, "value_vectors": value_vectors, "out_weight": out_weight, "window_start": window_start}


def attend_tile(query_tiles, key_grid, value_grid, window_start, tile_number):
    start_pair = window_start[tile_number]
    zero_index = jnp.zeros((), jnp.int32)
    corner = (start_pair[0].astype(jnp.int32), start_pair[1].astype(jnp.int32), zero_index, zero_index, zero_index)
    extent = (WT, WW, TILE, HEADS, DH)
    key_window = lax.dynamic_slice(key_grid, corner, extent).reshape(WT * WW * TILE, HEADS, DH).astype(jnp.float32)
    value_window = lax.dynamic_slice(value_grid, corner, extent).reshape(WT * WW * TILE, HEADS, DH).astype(jnp.float32)
    query_tile = query_tiles[tile_number].astype(jnp.float32)
    scores = jnp.einsum("qhd,khd->hqk", query_tile, key_window) * (DH ** -0.5)
    row_max = jnp.max(scores, axis=-1, keepdims=True)
    powers = jnp.exp(scores - row_max)
    totals = jnp.sum(powers, axis=-1)
    weights = lax.optimization_barrier(powers.astype(jnp.bfloat16)).astype(jnp.float32)
    mixed = jnp.einsum("hqk,khd->qhd", weights, value_window)
    return (mixed / jnp.transpose(totals)[:, :, None]).astype(jnp.bfloat16).reshape(TILE, HEADS * DH)


def reference(queries, key_vectors, value_vectors, out_weight, window_start):
    tile_total = SLABS * WTILES
    query_tiles = queries.reshape(tile_total, TILE, HEADS, DH)
    key_grid = key_vectors.reshape(SLABS, WTILES, TILE, HEADS, DH)
    value_grid = value_vectors.reshape(SLABS, WTILES, TILE, HEADS, DH)
    runner = partial(attend_tile, query_tiles, key_grid, value_grid, window_start)
    attended = lax.map(runner, jnp.arange(tile_total, dtype=jnp.int32)).reshape(TOKENS, HEADS * DH)
    group_width = HPD * DH

    def add_group(group_index, running):
        first = (group_index * group_width).astype(jnp.int32)
        columns = lax.dynamic_slice_in_dim(attended, first, group_width, 1)
        weight_rows = lax.dynamic_slice_in_dim(out_weight, first, group_width, 0)
        partial_sum = jnp.dot(columns, weight_rows, preferred_element_type=jnp.float32)
        rounded = lax.optimization_barrier(partial_sum.astype(jnp.bfloat16)).astype(jnp.float32)
        return running + rounded

    projected = lax.fori_loop(0, N_HEAD, add_group, jnp.zeros((TOKENS, HEADS * DH), jnp.float32))
    return projected.astype(jnp.bfloat16)
```

```python
import functools

import jax
import jax.numpy as jnp
from jax import lax
from jax.experimental import pallas as pl
from jax.experimental.pallas import tpu as pltpu
from jax.sharding import PartitionSpec as P

DH = 128
HPD = 3
ROW = 4
COLUMNS = 4
WINDOW = 3
RING = 4
HEAD_DEVICES = 8
MESH = pl.DeviceIdType.MESH


def attend(q_ref, k_ref, v_ref, o_ref, window, column, tile, factor):
    first = window[0, column]
    columns = pl.ds(window[1, column], WINDOW)
    rows = pl.ds(pl.multiple_of(column * tile, tile), tile)
    keys = (WINDOW * tile, DH)
    q = q_ref[rows, :]
    top = None
    for step in range(WINDOW):
        scores = lax.dot_general(
            q,
            k_ref[first + step, columns].reshape(keys),
            (((1,), (1,)), ((), ())),
            preferred_element_type=jnp.float32,
        )
        highest = jnp.max(scores, axis=-1, keepdims=True)
        if top is not None:
            highest = jnp.maximum(top, highest)
        powers = jnp.exp2((scores - highest) * factor)
        part = powers[:, :DH]
        for lane in range(DH, WINDOW * tile, DH):
            part = part + powers[:, lane : lane + DH]
        mixed = jnp.dot(
            powers.astype(jnp.bfloat16),
            v_ref[first + step, columns].reshape(keys),
            preferred_element_type=jnp.float32,
        )
        if top is None:
            total, acc = part, mixed
        else:
            fade = jnp.exp2((top - highest) * factor)
            total, acc = total * fade + part, acc * fade + mixed
        top = highest
    total = jnp.sum(total, axis=-1, keepdims=True)
    o_ref[rows, :] = (acc / total).astype(jnp.bfloat16)


def kernel(
    q_hbm, k_hbm, v_hbm, w_hbm, win_hbm, out_ref,
    k0, k1, k2, v0, v1, v2, q0, q1, q2, o0, o1, o2, a0, a1, a2, w0, w1, w2,
    acc, window,
    kv_recv, kv_send, q_recv, q_send, win_recv, win_send,
    w_own, w_recv, w_send, a_recv, a_send,
):
    ks, vs, qs, os_, as_, ws = (
        (k0, k1, k2), (v0, v1, v2), (q0, q1, q2), (o0, o1, o2), (a0, a1, a2), (w0, w1, w2),
    )
    kv = (ks, vs)
    kv_hbm = (k_hbm, v_hbm)
    tokens = q_hbm.shape[0]
    tile = tokens // COLUMNS
    piece = tokens // HEAD_DEVICES
    width = w_hbm.shape[1]
    factor = DH ** (-0.5) * 1.4426950408889634

    b = lax.axis_index("batch")
    s = lax.axis_index("seq")
    h = lax.axis_index("head")
    y, zh = s // ROW, s % ROW
    x, c = h // 2, h % 2
    g = zh // 2
    near = c == g
    far = c != g
    u = zh + g * (3 - 2 * zh)
    f = 1 - 2 * c
    spin = f * (1 - 2 * u)
    other = 2 * x + 1 - c
    zq = jnp.where(near, zh, 3 - zh)
    sq = ROW * y + zq
    hq = 2 * x + g
    y_next = (y - f + ROW) % ROW
    z_dev = (b, ROW * y + zh + 1 - 2 * (zh % 2), h)
    sib = (b, s, other)
    y_dev = (b, ROW * y_next + zh, other)
    b_dev = (b, jnp.where(u == 0, ROW * y_next + zh, s), other)
    partner_seq = ROW * y + 3 - zh
    partner = (b, partner_seq, other)
    xp, xm, xo = (x + 1) % RING, (x + 3) % RING, (x + 2) % RING
    xp_dev, xm_dev = (b, s, 2 * xp + c), (b, s, 2 * xm + c)

    def remote(src, dst, send, recv, device):
        return pltpu.make_async_remote_copy(
            src_ref=src, dst_ref=dst, send_sem=send, recv_sem=recv,
            device_id=device, device_id_type=MESH,
        )

    barrier = pltpu.get_barrier_semaphore()
    for hd in range(1, HEAD_DEVICES):
        pl.semaphore_signal(
            barrier, inc=1, device_id=(b, s, (h + hd) % HEAD_DEVICES), device_id_type=MESH
        )
    for hd in range(HEAD_DEVICES):
        pl.semaphore_signal(
            barrier, inc=1, device_id=(b, partner_seq, hd), device_id_type=MESH
        )
    pl.semaphore_signal(barrier, inc=1, device_id=z_dev, device_id_type=MESH)
    pl.semaphore_signal(barrier, inc=1, device_id=y_dev, device_id_type=MESH)
    pl.semaphore_wait(barrier, 2 * HEAD_DEVICES + 1)

    def head_columns(n):
        return pl.ds(n * DH, DH)

    def give(n, which):
        return remote(
            kv_hbm[which].at[:, :, head_columns(n)], kv[which][n].at[2],
            kv_send.at[n, which, 0], kv_recv.at[n, which, 2], partner,
        )

    def keep(n, which):
        return pltpu.make_async_copy(
            kv_hbm[which].at[:, :, head_columns(n)], kv[which][n].at[2], kv_recv.at[n, which, 2]
        )

    def give_q(n):
        return remote(q_hbm.at[:, head_columns(n)], qs[n], q_send.at[n], q_recv.at[n], partner)

    def keep_q(n):
        return pltpu.make_async_copy(q_hbm.at[:, head_columns(n)], qs[n], q_recv.at[n])

    give_win = remote(win_hbm, window, win_send, win_recv, partner)
    keep_win = pltpu.make_async_copy(win_hbm, window, win_recv)

    def relay(n, which, number):
        src, dst, device = (
            (2, 2 - spin, z_dev),
            (2, 2 + spin, b_dev),
            (2 + spin, 2 - 2 * f, sib),
            (2 + spin, 2 + 2 * f, y_dev),
        )[number]
        buf = kv[which][n]
        return remote(
            buf.at[src], buf.at[dst],
            kv_send.at[n, which, number + 1], kv_recv.at[n, which, dst], device,
        )

    def landed(n, which, slot):
        pltpu.make_async_copy(
            kv_hbm[which].at[:, :, head_columns(n)], kv[which][n].at[slot], kv_recv.at[n, which, slot]
        ).wait()

    def block(n, hd, first=0, count=DH):
        return ws[n].at[pl.ds(pl.multiple_of(hd * DH + first, 16), count), :]

    def own_rows(n):
        return w_hbm.at[pl.ds(n * DH, DH), :]

    half = DH // 2

    def w_copy(n, number):
        if number < 3:
            device = (xp_dev, xm_dev, sib)[number]
            recv = (0, 1, 4)[number]
            return remote(own_rows(n), block(n, h), w_send.at[n, number], w_recv.at[n, recv], device)
        if number == 3:
            part, recv, device = block(n, 2 * xm + c, 0, half), 2, xp_dev
        elif number == 4:
            part, recv, device = block(n, 2 * xp + c, half, half), 3, xm_dev
        else:
            part = block(n, 2 * (xm, xp, xo)[number - 5] + c)
            recv, device = number, sib
        return remote(part, part, w_send.at[n, number], w_recv.at[n, recv], device)

    def w_keep(n):
        return pltpu.make_async_copy(own_rows(n), block(n, h), w_own.at[n])

    def w_landed(n, recv):
        if recv < 2:
            part = block(n, 2 * (xm, xp)[recv] + c)
        elif recv == 2:
            part = block(n, 2 * xo + c, 0, half)
        elif recv == 3:
            part = block(n, 2 * xo + c, half, half)
        elif recv == 4:
            part = block(n, other)
        else:
            part = block(n, 2 * (xm, xp, xo)[recv - 5] + 1 - c)
        pltpu.make_async_copy(part, part, w_recv.at[n, recv]).wait()

    def w_second(n):
        w_landed(n, 0)
        w_copy(n, 3).start()
        w_copy(n, 5).start()
        w_landed(n, 1)
        w_copy(n, 4).start()
        w_copy(n, 6).start()

    def w_third(n):
        w_landed(n, 2)
        w_landed(n, 3)
        w_copy(n, 7).start()

    def first_relay(n):
        for which in range(2):
            landed(n, which, 2)
            relay(n, which, 0).start()
            relay(n, which, 1).start()

    def second_relay(n):
        for which in range(2):
            landed(n, which, 2 + spin)
            relay(n, which, 2).start()
            relay(n, which, 3).start()

    def o_rows(n, hd):
        return os_[n].at[pl.ds(pl.multiple_of(hd * piece, piece), piece), :]

    def o_place(n, head):
        return as_[n].at[:, pl.ds(pl.multiple_of(head * DH, DH), DH)]

    def o_copy(n, hd):
        return remote(
            o_rows(n, hd), o_place(n, hq), a_send.at[n, hd], a_recv.at[n, hq], (b, sq, hd)
        )

    def compute(n):
        for which in range(2):
            for slot in (2 - spin, 2 - 2 * f, 2 + 2 * f):
                landed(n, which, slot)
        keep_q(n).wait()

        @pl.loop(0, COLUMNS)
        def _(column):
            attend(qs[n], ks[n], vs[n], os_[n], window, column, tile, factor)
            for core in range(2):
                hd = 2 * column + core
                mine = jnp.logical_and(near, hd == h)

                @pl.when(mine)
                def _():
                    pltpu.make_async_copy(
                        o_rows(n, hd), o_place(n, hq), a_recv.at[n, hq]
                    ).start()

                @pl.when(jnp.logical_not(mine))
                def _():
                    o_copy(n, hd).start()

    chunk = 512

    def project(n):
        w_keep(n).wait()
        for recv in range(4, 8):
            w_landed(n, recv)
        for hd in range(HEAD_DEVICES):
            pltpu.make_async_copy(
                o_rows(n, hd), o_place(n, hd), a_recv.at[n, hd]
            ).wait()

        @pl.loop(0, width // chunk)
        def _(j):
            columns = pl.ds(pl.multiple_of(j * chunk, chunk), chunk)
            term = jnp.dot(as_[n][...], ws[n][:, columns], preferred_element_type=jnp.float32)
            if n == 0:
                acc[:, columns] = term
            elif n < HPD - 1:
                acc[:, columns] += term
            else:
                out_ref[:, columns] = (acc[:, columns] + term).astype(jnp.bfloat16)

    @pl.when(near)
    def _():
        keep_win.start()
        for n in range(HPD):
            keep(n, 0).start()
            keep(n, 1).start()
            keep_q(n).start()

    @pl.when(far)
    def _():
        give_win.start()
        for n in range(HPD):
            give(n, 0).start()
            give(n, 1).start()
            give_q(n).start()

    for n in range(HPD):
        w_keep(n).start()
        for number in range(3):
            w_copy(n, number).start()

    first_relay(0)
    w_second(0)
    second_relay(0)
    first_relay(1)
    keep_win.wait()
    w_third(0)
    compute(0)
    w_second(1)
    first_relay(2)
    second_relay(1)
    w_third(1)
    compute(1)
    w_second(2)
    project(0)
    second_relay(2)
    w_third(2)
    compute(2)
    project(1)
    project(2)

    for n in range(HPD):
        for which in range(2):
            for number in range(4):
                relay(n, which, number).wait_send()
        for number in range(8):
            w_copy(n, number).wait_send()
        for hd in range(HEAD_DEVICES):

            @pl.when(jnp.logical_not(jnp.logical_and(near, hd == h)))
            def _():
                o_copy(n, hd).wait_send()

    @pl.when(far)
    def _():
        give_win.wait_send()
        for n in range(HPD):
            give(n, 0).wait_send()
            give(n, 1).wait_send()
            give_q(n).wait_send()


def per_device(queries, key_vectors, value_vectors, out_weight, window_start):
    tokens = queries.shape[0]
    width = out_weight.shape[1]
    piece = tokens // HEAD_DEVICES
    half = jnp.bfloat16
    grid = (COLUMNS, tokens // COLUMNS, queries.shape[1])
    starts = window_start.T
    temporal = lax.broadcasted_iota(jnp.int32, starts.shape, 0) == 0
    window = starts - jnp.where(temporal, lax.axis_index("seq") - 2, 0)
    dma = pltpu.SemaphoreType.DMA
    scratch = (
        [pltpu.VMEM((5, COLUMNS, tokens // COLUMNS, DH), half)] * 6
        + [pltpu.VMEM((tokens, DH), half)] * 6
        + [pltpu.VMEM((piece, HEAD_DEVICES * DH), half)] * 3
        + [pltpu.VMEM((HEAD_DEVICES * DH, width), half)] * 3
        + [
            pltpu.VMEM((piece, width), jnp.float32),
            pltpu.SMEM(window.shape, jnp.int32),
            dma((HPD, 2, 5)), dma((HPD, 2, 5)), dma((HPD,)), dma((HPD,)), dma, dma,
            dma((HPD,)), dma((HPD, 8)), dma((HPD, 8)),
            dma((HPD, HEAD_DEVICES)), dma((HPD, HEAD_DEVICES)),
        ]
    )
    return pl.pallas_call(
        kernel,
        out_shape=jax.ShapeDtypeStruct((piece, width), half),
        in_specs=[pl.BlockSpec(memory_space=pl.ANY)] * 5,
        out_specs=pl.BlockSpec(memory_space=pltpu.VMEM),
        scratch_shapes=scratch,
        compiler_params=pltpu.CompilerParams(
            collective_id=0, has_side_effects=True, vmem_limit_bytes=60 * 1024 * 1024
        ),
    )(
        queries, key_vectors.reshape(grid), value_vectors.reshape(grid), out_weight, window
    )


def solution(mesh):
    in_specs = (
        P(("batch", "seq"), "head"),
        P(("batch", "seq"), "head"),
        P(("batch", "seq"), "head"),
        P("head", None),
        P(("batch", "seq"), None),
    )
    out_specs = P(("batch", "seq", "head"), None)
    return jax.shard_map(
        per_device, mesh=mesh, in_specs=in_specs, out_specs=out_specs, check_vma=False
    )
```

```python
import functools

import jax
import jax.numpy as jnp
from jax import lax
from jax.experimental import pallas as pl
from jax.experimental.pallas import tpu as pltpu
from jax.sharding import PartitionSpec as P

DH = 128
HPD = 3
ROW = 4
COLUMNS = 4
WINDOW = 3
RING = 4
HEAD_DEVICES = 8
PIECES = 2
SLOTS = 5
MESH = pl.DeviceIdType.MESH


def keys_of(ref, window, column, step):
    slot = lax.rem(window[0, column] + step, SLOTS)
    rows = ref[slot, pl.ds(window[1, column], WINDOW)]
    return rows.reshape(rows.shape[0] * rows.shape[1], DH)


def scores_of(q, ref, window, column, step):
    return lax.dot_general(
        q,
        keys_of(ref, window, column, step),
        (((1,), (1,)), ((), ())),
        preferred_element_type=jnp.float32,
    )


def lane_sums(powers):
    part = powers[:, :DH]
    for lane in range(DH, powers.shape[1], DH):
        part = part + powers[:, lane : lane + DH]
    return part


def attend(q_ref, k_ref, v_ref, o_ref, window, column, tile, factor):
    rows = pl.ds(pl.multiple_of(column * tile, tile), tile)
    q = q_ref[rows, :]
    top = None
    for step in range(WINDOW):
        scores = scores_of(q, k_ref, window, column, step)
        highest = jnp.max(scores, axis=-1, keepdims=True)
        if top is not None:
            highest = jnp.maximum(top, highest)
        powers = jnp.exp2((scores - highest) * factor)
        part = lane_sums(powers)
        mixed = jnp.dot(
            powers.astype(jnp.bfloat16),
            keys_of(v_ref, window, column, step),
            preferred_element_type=jnp.float32,
        )
        if top is None:
            total, acc = part, mixed
        else:
            fade = jnp.exp2((top - highest) * factor)
            total, acc = total * fade + part, acc * fade + mixed
        top = highest
    total = jnp.sum(total, axis=-1, keepdims=True)
    o_ref[rows, :] = (acc / total).astype(jnp.bfloat16)


def weigh(q_ref, k_ref, weights, totals, window, column, tile, factor):
    rows = pl.ds(pl.multiple_of(column * tile, tile), tile)
    q = q_ref[rows, :]
    scores = [scores_of(q, k_ref, window, column, step) for step in range(WINDOW)]
    highest = functools.reduce(
        jnp.maximum, [jnp.max(term, axis=-1, keepdims=True) for term in scores]
    )
    total = None
    for step in range(WINDOW):
        powers = jnp.exp2((scores[step] - highest) * factor)
        part = lane_sums(powers)
        total = part if total is None else total + part
        weights[column, step] = powers.astype(jnp.bfloat16)
    totals[rows, :] = total


def mix(v_ref, o_ref, weights, totals, window, column, tile):
    rows = pl.ds(pl.multiple_of(column * tile, tile), tile)
    acc = None
    for step in range(WINDOW):
        mixed = jnp.dot(
            weights[column, step],
            keys_of(v_ref, window, column, step),
            preferred_element_type=jnp.float32,
        )
        acc = mixed if acc is None else acc + mixed
    total = jnp.sum(totals[rows, :], axis=-1, keepdims=True)
    o_ref[rows, :] = (acc / total).astype(jnp.bfloat16)


def kernel(
    q_hbm, k_hbm, v_hbm, w_hbm, win_hbm, out_ref,
    k0, k1, k2, v0, v1, v2, q0, q1, q2, o0, o1, o2, a0, a1, a2, w0, w1, w2,
    acc, weights, totals, window,
    kv_recv, kv_send, q_recv, q_send, win_recv, win_send,
    w_own, w_recv, w_send, a_recv, a_send, row_open,
):
    ks, vs, qs, os_, as_, ws = (
        (k0, k1, k2), (v0, v1, v2), (q0, q1, q2), (o0, o1, o2), (a0, a1, a2), (w0, w1, w2),
    )
    kv = (ks, vs)
    kv_hbm = (k_hbm, v_hbm)
    tokens = q_hbm.shape[0]
    tile = tokens // COLUMNS
    piece = tokens // HEAD_DEVICES
    width = w_hbm.shape[1]
    factor = DH ** (-0.5) * 1.4426950408889634

    b = lax.axis_index("batch")
    s = lax.axis_index("seq")
    h = lax.axis_index("head")
    y, zh = s // ROW, s % ROW
    x, c = h // 2, h % 2
    g = zh // 2
    near = c == g
    far = c != g
    u = zh + g * (3 - 2 * zh)
    f = 1 - 2 * c
    spin = f * (1 - 2 * u)
    other = 2 * x + 1 - c
    zq = jnp.where(near, zh, 3 - zh)
    sq = ROW * y + zq
    hq = 2 * x + g
    y_next = (y - f + ROW) % ROW
    z_dev = (b, ROW * y + zh + 1 - 2 * (zh % 2), h)
    sib = (b, s, other)
    y_dev = (b, ROW * y_next + zh, other)
    b_dev = (b, jnp.where(u == 0, ROW * y_next + zh, s), other)
    partner_seq = ROW * y + 3 - zh
    partner = (b, partner_seq, other)
    xp, xm, xo = (x + 1) % RING, (x + 3) % RING, (x + 2) % RING
    xp_dev, xm_dev = (b, s, 2 * xp + c), (b, s, 2 * xm + c)

    def remote(src, dst, send, recv, device):
        return pltpu.make_async_remote_copy(
            src_ref=src, dst_ref=dst, send_sem=send, recv_sem=recv,
            device_id=device, device_id_type=MESH,
        )

    barrier = pltpu.get_barrier_semaphore()
    for device in (z_dev, y_dev, sib, xp_dev, xm_dev):
        pl.semaphore_signal(barrier, inc=1, device_id=device, device_id_type=MESH)

    @pl.when(far)
    def _():
        pl.semaphore_signal(barrier, inc=1, device_id=partner, device_id_type=MESH)

    pl.semaphore_wait(barrier, jnp.where(far, 6, 5))

    def slot_of(first, offset):
        return (first + offset + SLOTS) % SLOTS

    own = slot_of(sq, 0)
    given = slot_of(s, 0)
    crossed = slot_of(sq, spin)
    y_first = ROW * y_next + 3 - zq

    def head_columns(n):
        return pl.ds(n * DH, DH)

    def part(p):
        count = COLUMNS // PIECES
        return pl.ds(p * count, count)

    def give(n, which, p):
        return remote(
            kv_hbm[which].at[part(p), :, head_columns(n)], kv[which][n].at[given, part(p)],
            kv_send.at[n, which, 0, p], kv_recv.at[n, which, given, p], partner,
        )

    def keep(n, which, p):
        return pltpu.make_async_copy(
            kv_hbm[which].at[part(p), :, head_columns(n)],
            kv[which][n].at[own, part(p)],
            kv_recv.at[n, which, own, p],
        )

    def give_q(n):
        return remote(q_hbm.at[:, head_columns(n)], qs[n], q_send.at[n], q_recv.at[n], partner)

    def keep_q(n):
        return pltpu.make_async_copy(q_hbm.at[:, head_columns(n)], qs[n], q_recv.at[n])

    give_win = remote(win_hbm, window, win_send, win_recv, partner)
    keep_win = pltpu.make_async_copy(win_hbm, window, win_recv)

    def relay(n, which, number, p):
        src, dst, device = (
            (own, own, z_dev),
            (own, jnp.where(u == 0, slot_of(y_first, f), own), b_dev),
            (crossed, crossed, sib),
            (crossed, slot_of(y_first, 2 * f), y_dev),
        )[number]
        buf = kv[which][n]
        return remote(
            buf.at[src, part(p)], buf.at[dst, part(p)],
            kv_send.at[n, which, number + 1, p], kv_recv.at[n, which, dst, p], device,
        )

    def landed(n, which, slot, p):
        pltpu.make_async_copy(
            kv_hbm[which].at[part(p), :, head_columns(n)],
            kv[which][n].at[slot, part(p)],
            kv_recv.at[n, which, slot, p],
        ).wait()

    def block(n, hd, first=0, count=DH):
        return ws[n].at[pl.ds(pl.multiple_of(hd * DH + first, 16), count), :]

    def own_rows(n):
        return w_hbm.at[pl.ds(n * DH, DH), :]

    half = DH // 2

    def w_copy(n, number):
        if number < 3:
            device = (xp_dev, xm_dev, sib)[number]
            recv = (0, 1, 4)[number]
            return remote(own_rows(n), block(n, h), w_send.at[n, number], w_recv.at[n, recv], device)
        if number == 3:
            part, recv, device = block(n, 2 * xm + c, 0, half), 2, xp_dev
        elif number == 4:
            part, recv, device = block(n, 2 * xp + c, half, half), 3, xm_dev
        else:
            part = block(n, 2 * (xm, xp, xo)[number - 5] + c)
            recv, device = number, sib
        return remote(part, part, w_send.at[n, number], w_recv.at[n, recv], device)

    def w_keep(n):
        return pltpu.make_async_copy(own_rows(n), block(n, h), w_own.at[n])

    def w_landed(n, recv):
        if recv < 2:
            part = block(n, 2 * (xm, xp)[recv] + c)
        elif recv == 2:
            part = block(n, 2 * xo + c, 0, half)
        elif recv == 3:
            part = block(n, 2 * xo + c, half, half)
        elif recv == 4:
            part = block(n, other)
        else:
            part = block(n, 2 * (xm, xp, xo)[recv - 5] + 1 - c)
        pltpu.make_async_copy(part, part, w_recv.at[n, recv]).wait()

    def w_second(n):
        w_landed(n, 0)
        w_copy(n, 3).start()
        w_copy(n, 5).start()
        w_landed(n, 1)
        w_copy(n, 4).start()
        w_copy(n, 6).start()

    def w_third(n):
        w_landed(n, 2)
        w_landed(n, 3)
        w_copy(n, 7).start()

    def w_all(n):
        for recv in range(4, 8):
            w_landed(n, recv)

    def first_relay(n):
        for which in range(2):
            for p in range(PIECES):
                landed(n, which, own, p)
                relay(n, which, 0, p).start()
                relay(n, which, 1, p).start()

    def second_relay(n, which):
        for p in range(PIECES):
            landed(n, which, crossed, p)
            relay(n, which, 3, p).start()
            relay(n, which, 2, p).start()

    def o_rows(n, hd):
        return os_[n].at[pl.ds(pl.multiple_of(hd * piece, piece), piece), :]

    def o_place(n, head):
        return as_[n].at[:, pl.ds(pl.multiple_of(head * DH, DH), DH)]

    def o_copy(n, hd):
        return remote(
            o_rows(n, hd), o_place(n, hq), a_send.at[n, hd], a_recv.at[n, hq], (b, sq, hd)
        )

    def all_landed(n, which):
        for offset in (-spin, -2 * f, 2 * f):
            for p in range(PIECES):
                landed(n, which, slot_of(sq, offset), p)

    def send_rows(n, column):
        for core in range(2):
            hd = 2 * column + core
            mine = jnp.logical_and(near, hd == h)

            @pl.when(mine)
            def _():
                pltpu.make_async_copy(
                    o_rows(n, hd), o_place(n, hq), a_recv.at[n, hq]
                ).start()

            @pl.when(jnp.logical_not(mine))
            def _():
                o_copy(n, hd).start()

    def compute(n):
        all_landed(n, 0)
        all_landed(n, 1)
        keep_q(n).wait()

        @pl.loop(0, COLUMNS)
        def _(column):
            attend(qs[n], ks[n], vs[n], os_[n], window, column, tile, factor)
            send_rows(n, column)

    def compute_weights(n):
        all_landed(n, 0)
        keep_q(n).wait()

        @pl.loop(0, COLUMNS)
        def _(column):
            weigh(qs[n], ks[n], weights, totals, window, column, tile, factor)

    def compute_mix(n):
        all_landed(n, 1)

        @pl.loop(0, COLUMNS)
        def _(column):
            mix(vs[n], os_[n], weights, totals, window, column, tile)
            send_rows(n, column)

    chunk = 512

    def project(n):
        w_keep(n).wait()
        if n > 0:
            w_all(n)
        for hd in range(HEAD_DEVICES):
            pltpu.make_async_copy(
                o_rows(n, hd), o_place(n, hd), a_recv.at[n, hd]
            ).wait()

        @pl.loop(0, width // chunk)
        def _(j):
            columns = pl.ds(pl.multiple_of(j * chunk, chunk), chunk)
            term = jnp.dot(as_[n][...], ws[n][:, columns], preferred_element_type=jnp.float32)
            if n == 0:
                acc[:, columns] = term
            elif n < HPD - 1:
                acc[:, columns] += term
            else:
                out_ref[:, columns] = (acc[:, columns] + term).astype(jnp.bfloat16)

    @pl.when(near)
    def _():
        keep_win.start()
        for n in range(HPD):
            for which in range(2):
                for p in range(PIECES):
                    keep(n, which, p).start()
        for n in range(HPD):
            keep_q(n).start()

    @pl.when(far)
    def _():
        for n in range(HPD):
            for which in range(2):
                for p in range(PIECES):
                    give(n, which, p).start()
            if n == 0:
                give_q(n).start()
                give_win.start()
        for n in range(1, HPD):
            give_q(n).start()

    for n in range(HPD):
        w_keep(n).start()
        for number in range(3):
            w_copy(n, number).start()

    @pl.when(near)
    def _():
        for n in range(HPD):
            first_relay(n)

    @pl.when(far)
    def _():
        first_relay(0)

    w_second(0)

    @pl.when(far)
    def _():
        first_relay(1)

    second_relay(0, 0)
    second_relay(0, 1)
    keep_win.wait()
    w_third(0)
    w_all(0)

    @pl.when(far)
    def _():
        pl.semaphore_signal(row_open, inc=1, device_id=partner, device_id_type=MESH)
        pl.semaphore_wait(row_open, 1)

    compute(0)
    w_second(1)

    @pl.when(far)
    def _():
        first_relay(2)

    second_relay(1, 0)
    second_relay(1, 1)
    w_third(1)
    compute(1)
    w_second(2)
    second_relay(2, 0)
    project(0)
    w_third(2)
    compute_weights(2)
    second_relay(2, 1)
    project(1)
    compute_mix(2)
    project(2)

    for n in range(HPD):
        for which in range(2):
            for number in range(4):
                for p in range(PIECES):
                    relay(n, which, number, p).wait_send()
        for number in range(8):
            w_copy(n, number).wait_send()
        for hd in range(HEAD_DEVICES):

            @pl.when(jnp.logical_not(jnp.logical_and(near, hd == h)))
            def _():
                o_copy(n, hd).wait_send()

    @pl.when(far)
    def _():
        give_win.wait_send()
        for n in range(HPD):
            for which in range(2):
                for p in range(PIECES):
                    give(n, which, p).wait_send()
            give_q(n).wait_send()


def per_device(queries, key_vectors, value_vectors, out_weight, window_start):
    tokens = queries.shape[0]
    width = out_weight.shape[1]
    piece = tokens // HEAD_DEVICES
    half = jnp.bfloat16
    grid = (COLUMNS, tokens // COLUMNS, queries.shape[1])
    window = window_start.T
    dma = pltpu.SemaphoreType.DMA
    scratch = (
        [pltpu.VMEM((5, COLUMNS, tokens // COLUMNS, DH), half)] * 6
        + [pltpu.VMEM((tokens, DH), half)] * 6
        + [pltpu.VMEM((piece, HEAD_DEVICES * DH), half)] * 3
        + [pltpu.VMEM((HEAD_DEVICES * DH, width), half)] * 3
        + [
            pltpu.VMEM((piece, width), jnp.float32),
            pltpu.VMEM((COLUMNS, WINDOW, tokens // COLUMNS, WINDOW * tokens // COLUMNS), half),
            pltpu.VMEM((tokens, DH), jnp.float32),
            pltpu.SMEM(window.shape, jnp.int32),
            dma((HPD, 2, 5, PIECES)), dma((HPD, 2, 5, PIECES)), dma((HPD,)), dma((HPD,)), dma, dma,
            dma((HPD,)), dma((HPD, 8)), dma((HPD, 8)),
            dma((HPD, HEAD_DEVICES)), dma((HPD, HEAD_DEVICES)), pltpu.SemaphoreType.REGULAR,
        ]
    )
    return pl.pallas_call(
        kernel,
        out_shape=jax.ShapeDtypeStruct((piece, width), half),
        in_specs=[pl.BlockSpec(memory_space=pl.ANY)] * 5,
        out_specs=pl.BlockSpec(memory_space=pltpu.VMEM),
        scratch_shapes=scratch,
        compiler_params=pltpu.CompilerParams(
            collective_id=0, has_side_effects=True, vmem_limit_bytes=60 * 1024 * 1024
        ),
    )(
        queries, key_vectors.reshape(grid), value_vectors.reshape(grid), out_weight, window
    )


def solution(mesh):
    in_specs = (
        P(("batch", "seq"), "head"),
        P(("batch", "seq"), "head"),
        P(("batch", "seq"), "head"),
        P("head", None),
        P(("batch", "seq"), None),
    )
    out_specs = P(("batch", "seq", "head"), None)
    return jax.shard_map(
        per_device, mesh=mesh, in_specs=in_specs, out_specs=out_specs, check_vma=False
    )
```

```python
import functools

import jax
import jax.numpy as jnp
from jax import lax
from jax.experimental import pallas as pl
from jax.experimental.pallas import tpu as pltpu
from jax.sharding import PartitionSpec as P

DH = 128
HPD = 3
ROW = 4
COLUMNS = 4
WINDOW = 3
RING = 4
HEAD_DEVICES = 8
PIECES = 2
GATE = (0, 0)
SLOTS = 5
MESH = pl.DeviceIdType.MESH


def keys_of(ref, window, column, step):
    slot = lax.rem(window[0, column] + step, SLOTS)
    rows = ref[slot, pl.ds(window[1, column], WINDOW)]
    return rows.reshape(rows.shape[0] * rows.shape[1], DH)


def scores_of(q, ref, window, column, step):
    return lax.dot_general(
        q,
        keys_of(ref, window, column, step),
        (((1,), (1,)), ((), ())),
        preferred_element_type=jnp.float32,
    )


def lane_sums(powers):
    part = powers[:, :DH]
    for lane in range(DH, powers.shape[1], DH):
        part = part + powers[:, lane : lane + DH]
    return part


def attend(q_ref, k_ref, v_ref, o_ref, window, column, tile, factor):
    rows = pl.ds(pl.multiple_of(column * tile, tile), tile)
    q = q_ref[rows, :]
    top = None
    for step in range(WINDOW):
        scores = scores_of(q, k_ref, window, column, step)
        highest = jnp.max(scores, axis=-1, keepdims=True)
        if top is not None:
            highest = jnp.maximum(top, highest)
        powers = jnp.exp2((scores - highest) * factor)
        part = lane_sums(powers)
        mixed = jnp.dot(
            powers.astype(jnp.bfloat16),
            keys_of(v_ref, window, column, step),
            preferred_element_type=jnp.float32,
        )
        if top is None:
            total, acc = part, mixed
        else:
            fade = jnp.exp2((top - highest) * factor)
            total, acc = total * fade + part, acc * fade + mixed
        top = highest
    total = jnp.sum(total, axis=-1, keepdims=True)
    o_ref[rows, :] = (acc / total).astype(jnp.bfloat16)


def weigh(q_ref, k_ref, weights, totals, window, column, tile, factor):
    rows = pl.ds(pl.multiple_of(column * tile, tile), tile)
    q = q_ref[rows, :]
    scores = [scores_of(q, k_ref, window, column, step) for step in range(WINDOW)]
    highest = functools.reduce(
        jnp.maximum, [jnp.max(term, axis=-1, keepdims=True) for term in scores]
    )
    total = None
    for step in range(WINDOW):
        powers = jnp.exp2((scores[step] - highest) * factor)
        part = lane_sums(powers)
        total = part if total is None else total + part
        weights[column, step] = powers.astype(jnp.bfloat16)
    totals[rows, :] = total


def mix(v_ref, o_ref, weights, totals, window, column, tile):
    rows = pl.ds(pl.multiple_of(column * tile, tile), tile)
    acc = None
    for step in range(WINDOW):
        mixed = jnp.dot(
            weights[column, step],
            keys_of(v_ref, window, column, step),
            preferred_element_type=jnp.float32,
        )
        acc = mixed if acc is None else acc + mixed
    total = jnp.sum(totals[rows, :], axis=-1, keepdims=True)
    o_ref[rows, :] = (acc / total).astype(jnp.bfloat16)


def kernel(
    q_hbm, k_hbm, v_hbm, w_hbm, win_hbm, out_ref,
    k0, k1, k2, v0, v1, v2, q0, q1, q2, o0, o1, o2, a0, a1, a2, w0, w1, w2,
    acc, weights, totals, window,
    kv_recv, kv_send, q_recv, q_send, win_recv, win_send,
    w_own, w_recv, w_send, a_recv, a_send, row_open,
):
    ks, vs, qs, os_, as_, ws = (
        (k0, k1, k2), (v0, v1, v2), (q0, q1, q2), (o0, o1, o2), (a0, a1, a2), (w0, w1, w2),
    )
    kv = (ks, vs)
    kv_hbm = (k_hbm, v_hbm)
    tokens = q_hbm.shape[0]
    tile = tokens // COLUMNS
    piece = tokens // HEAD_DEVICES
    width = w_hbm.shape[1]
    factor = DH ** (-0.5) * 1.4426950408889634

    b = lax.axis_index("batch")
    s = lax.axis_index("seq")
    h = lax.axis_index("head")
    y, zh = s // ROW, s % ROW
    x, c = h // 2, h % 2
    g = zh // 2
    near = c == g
    far = c != g
    u = zh + g * (3 - 2 * zh)
    f = 1 - 2 * c
    spin = f * (1 - 2 * u)
    other = 2 * x + 1 - c
    zq = jnp.where(near, zh, 3 - zh)
    sq = ROW * y + zq
    hq = 2 * x + g
    y_next = (y - f + ROW) % ROW
    z_dev = (b, ROW * y + zh + 1 - 2 * (zh % 2), h)
    sib = (b, s, other)
    y_dev = (b, ROW * y_next + zh, other)
    b_dev = (b, jnp.where(u == 0, ROW * y_next + zh, s), other)
    partner_seq = ROW * y + 3 - zh
    partner = (b, partner_seq, other)
    xp, xm, xo = (x + 1) % RING, (x + 3) % RING, (x + 2) % RING
    xp_dev, xm_dev = (b, s, 2 * xp + c), (b, s, 2 * xm + c)

    def remote(src, dst, send, recv, device):
        return pltpu.make_async_remote_copy(
            src_ref=src, dst_ref=dst, send_sem=send, recv_sem=recv,
            device_id=device, device_id_type=MESH,
        )

    barrier = pltpu.get_barrier_semaphore()
    for device in (z_dev, y_dev, sib, xp_dev, xm_dev):
        pl.semaphore_signal(barrier, inc=1, device_id=device, device_id_type=MESH)

    @pl.when(far)
    def _():
        pl.semaphore_signal(barrier, inc=1, device_id=partner, device_id_type=MESH)

    pl.semaphore_wait(barrier, jnp.where(far, 6, 5))
    for device in (sib, xp_dev, xm_dev):
        pl.semaphore_signal(row_open.at[0], inc=1, device_id=device, device_id_type=MESH)

    def slot_of(first, offset):
        return (first + offset + SLOTS) % SLOTS

    own = slot_of(sq, 0)
    given = slot_of(s, 0)
    crossed = slot_of(sq, spin)
    y_first = ROW * y_next + 3 - zq

    def head_columns(n):
        return pl.ds(n * DH, DH)

    def part(p):
        count = COLUMNS // PIECES
        return pl.ds(p * count, count)

    def give(n, which, p):
        return remote(
            kv_hbm[which].at[part(p), :, head_columns(n)], kv[which][n].at[given, part(p)],
            kv_send.at[n, which, 0, p], kv_recv.at[n, which, given, p], partner,
        )

    def keep(n, which, p):
        return pltpu.make_async_copy(
            kv_hbm[which].at[part(p), :, head_columns(n)],
            kv[which][n].at[own, part(p)],
            kv_recv.at[n, which, own, p],
        )

    def give_q(n):
        return remote(q_hbm.at[:, head_columns(n)], qs[n], q_send.at[n], q_recv.at[n], partner)

    def keep_q(n):
        return pltpu.make_async_copy(q_hbm.at[:, head_columns(n)], qs[n], q_recv.at[n])

    give_win = remote(win_hbm, window, win_send, win_recv, partner)
    keep_win = pltpu.make_async_copy(win_hbm, window, win_recv)

    def relay(n, which, number, p):
        src, dst, device = (
            (own, own, z_dev),
            (own, jnp.where(u == 0, slot_of(y_first, f), own), b_dev),
            (crossed, crossed, sib),
            (crossed, slot_of(y_first, 2 * f), y_dev),
        )[number]
        buf = kv[which][n]
        return remote(
            buf.at[src, part(p)], buf.at[dst, part(p)],
            kv_send.at[n, which, number + 1, p], kv_recv.at[n, which, dst, p], device,
        )

    def landed(n, which, slot, p):
        pltpu.make_async_copy(
            kv_hbm[which].at[part(p), :, head_columns(n)],
            kv[which][n].at[slot, part(p)],
            kv_recv.at[n, which, slot, p],
        ).wait()

    def block(n, hd, first=0, count=DH):
        return ws[n].at[pl.ds(pl.multiple_of(hd * DH + first, 16), count), :]

    def own_rows(n):
        return w_hbm.at[pl.ds(n * DH, DH), :]

    half = DH // 2

    def w_copy(n, number):
        if number < 3:
            device = (xp_dev, xm_dev, sib)[number]
            recv = (0, 1, 4)[number]
            return remote(own_rows(n), block(n, h), w_send.at[n, number], w_recv.at[n, recv], device)
        if number == 3:
            part, recv, device = block(n, 2 * xm + c, 0, half), 2, xp_dev
        elif number == 4:
            part, recv, device = block(n, 2 * xp + c, half, half), 3, xm_dev
        else:
            part = block(n, 2 * (xm, xp, xo)[number - 5] + c)
            recv, device = number, sib
        return remote(part, part, w_send.at[n, number], w_recv.at[n, recv], device)

    def w_keep(n):
        return pltpu.make_async_copy(own_rows(n), block(n, h), w_own.at[n])

    def w_landed(n, recv):
        if recv < 2:
            part = block(n, 2 * (xm, xp)[recv] + c)
        elif recv == 2:
            part = block(n, 2 * xo + c, 0, half)
        elif recv == 3:
            part = block(n, 2 * xo + c, half, half)
        elif recv == 4:
            part = block(n, other)
        else:
            part = block(n, 2 * (xm, xp, xo)[recv - 5] + 1 - c)
        pltpu.make_async_copy(part, part, w_recv.at[n, recv]).wait()

    def w_second(n):
        w_landed(n, 0)
        w_copy(n, 3).start()
        w_copy(n, 5).start()
        w_landed(n, 1)
        w_copy(n, 4).start()
        w_copy(n, 6).start()

    def w_third(n):
        w_landed(n, 2)
        w_landed(n, 3)
        w_copy(n, 7).start()

    def w_all(n):
        for recv in range(4, 8):
            w_landed(n, recv)

    def first_relay(n):
        for which in range(2):
            for p in range(PIECES):
                landed(n, which, own, p)
                relay(n, which, 0, p).start()
                relay(n, which, 1, p).start()

    def second_relay(n, which):
        for p in range(PIECES):
            landed(n, which, crossed, p)
            relay(n, which, 3, p).start()
            relay(n, which, 2, p).start()

    def o_rows(n, hd):
        return os_[n].at[pl.ds(pl.multiple_of(hd * piece, piece), piece), :]

    def o_place(n, head):
        return as_[n].at[:, pl.ds(pl.multiple_of(head * DH, DH), DH)]

    def o_copy(n, hd):
        return remote(
            o_rows(n, hd), o_place(n, hq), a_send.at[n, hd], a_recv.at[n, hq], (b, sq, hd)
        )

    def all_landed(n, which):
        for offset in (-spin, -2 * f):
            for p in range(PIECES):
                landed(n, which, slot_of(sq, offset), p)

        @pl.when(near if (n, which) == GATE else near | far)
        def _():
            for p in range(PIECES):
                landed(n, which, slot_of(sq, 2 * f), p)

    def send_rows(n, column):
        for core in range(2):
            hd = 2 * column + core
            mine = jnp.logical_and(near, hd == h)

            @pl.when(mine)
            def _():
                pltpu.make_async_copy(
                    o_rows(n, hd), o_place(n, hq), a_recv.at[n, hq]
                ).start()

            @pl.when(jnp.logical_not(mine))
            def _():
                o_copy(n, hd).start()

    def compute(n):
        all_landed(n, 0)
        all_landed(n, 1)
        keep_q(n).wait()

        @pl.loop(0, COLUMNS)
        def _(column):
            attend(qs[n], ks[n], vs[n], os_[n], window, column, tile, factor)
            send_rows(n, column)

    def compute_weights(n):
        all_landed(n, 0)
        keep_q(n).wait()

        @pl.loop(0, COLUMNS)
        def _(column):
            weigh(qs[n], ks[n], weights, totals, window, column, tile, factor)

    def compute_mix(n):
        all_landed(n, 1)

        @pl.loop(0, COLUMNS)
        def _(column):
            mix(vs[n], os_[n], weights, totals, window, column, tile)
            send_rows(n, column)

    chunk = 512

    def project(n):
        w_keep(n).wait()
        w_all(n)
        for hd in range(HEAD_DEVICES):
            pltpu.make_async_copy(
                o_rows(n, hd), o_place(n, hd), a_recv.at[n, hd]
            ).wait()

        @pl.loop(0, width // chunk)
        def _(j):
            columns = pl.ds(pl.multiple_of(j * chunk, chunk), chunk)
            term = jnp.dot(as_[n][...], ws[n][:, columns], preferred_element_type=jnp.float32)
            if n == 0:
                acc[:, columns] = term
            elif n < HPD - 1:
                acc[:, columns] += term
            else:
                out_ref[:, columns] = (acc[:, columns] + term).astype(jnp.bfloat16)

    @pl.when(near)
    def _():
        keep_win.start()
        for n in range(HPD):
            for which in range(2):
                for p in range(PIECES):
                    keep(n, which, p).start()
        for n in range(HPD):
            keep_q(n).start()

    @pl.when(far)
    def _():
        for n in range(HPD):
            for which in range(2):
                for p in range(PIECES):
                    give(n, which, p).start()
            if n == 0:
                give_q(n).start()
                give_win.start()
        for n in range(1, HPD):
            give_q(n).start()

    for n in range(HPD):
        w_keep(n).start()
        for number in range(3):
            w_copy(n, number).start()

    @pl.when(near)
    def _():
        first_relay(0)
        first_relay(1)
        first_relay(2)

    pl.semaphore_wait(row_open.at[0], 3)
    pl.semaphore_signal(row_open.at[1], inc=1, device_id=sib, device_id_type=MESH)
    w_second(0)
    @pl.when(near)
    def _():
        second_relay(0, 0)
        second_relay(0, 1)

    @pl.when(far)
    def _():
        for p in range(PIECES):
            landed(0, 0, slot_of(sq, 2 * f), p)
        first_relay(0)

    w_second(1)
    @pl.when(near)
    def _():
        second_relay(1, 0)
        second_relay(1, 1)

    @pl.when(far)
    def _():
        first_relay(1)
        second_relay(0, 0)
        second_relay(0, 1)

    pl.semaphore_wait(row_open.at[1], 1)

    @pl.when(far)
    def _():
        pl.semaphore_signal(row_open.at[2], inc=1, device_id=partner, device_id_type=MESH)

    keep_win.wait()

    @pl.when(far)
    def _():
        pl.semaphore_wait(row_open.at[2], 1)

    compute(0)
    w_second(2)
    @pl.when(near)
    def _():
        second_relay(2, 0)
        second_relay(2, 1)

    @pl.when(far)
    def _():
        first_relay(2)

    w_third(0)
    @pl.when(far)
    def _():
        second_relay(1, 0)
        second_relay(1, 1)

    w_third(1)
    compute(1)
    @pl.when(far)
    def _():
        second_relay(2, 0)

    w_third(2)
    compute_weights(2)
    @pl.when(far)
    def _():
        second_relay(2, 1)

    project(0)
    project(1)
    compute_mix(2)
    project(2)

    for n in range(HPD):
        for which in range(2):
            for number in range(4):
                for p in range(PIECES):
                    relay(n, which, number, p).wait_send()
        for number in range(8):
            w_copy(n, number).wait_send()
        for hd in range(HEAD_DEVICES):

            @pl.when(jnp.logical_not(jnp.logical_and(near, hd == h)))
            def _():
                o_copy(n, hd).wait_send()

    @pl.when(far)
    def _():
        give_win.wait_send()
        for n in range(HPD):
            for which in range(2):
                for p in range(PIECES):
                    give(n, which, p).wait_send()
            give_q(n).wait_send()


def per_device(queries, key_vectors, value_vectors, out_weight, window_start):
    tokens = queries.shape[0]
    width = out_weight.shape[1]
    piece = tokens // HEAD_DEVICES
    half = jnp.bfloat16
    grid = (COLUMNS, tokens // COLUMNS, queries.shape[1])
    window = window_start.T
    dma = pltpu.SemaphoreType.DMA
    scratch = (
        [pltpu.VMEM((5, COLUMNS, tokens // COLUMNS, DH), half)] * 6
        + [pltpu.VMEM((tokens, DH), half)] * 6
        + [pltpu.VMEM((piece, HEAD_DEVICES * DH), half)] * 3
        + [pltpu.VMEM((HEAD_DEVICES * DH, width), half)] * 3
        + [
            pltpu.VMEM((piece, width), jnp.float32),
            pltpu.VMEM((COLUMNS, WINDOW, tokens // COLUMNS, WINDOW * tokens // COLUMNS), half),
            pltpu.VMEM((tokens, DH), jnp.float32),
            pltpu.SMEM(window.shape, jnp.int32),
            dma((HPD, 2, 5, PIECES)), dma((HPD, 2, 5, PIECES)), dma((HPD,)), dma((HPD,)), dma, dma,
            dma((HPD,)), dma((HPD, 8)), dma((HPD, 8)),
            dma((HPD, HEAD_DEVICES)), dma((HPD, HEAD_DEVICES)), pltpu.SemaphoreType.REGULAR((3,)),
        ]
    )
    return pl.pallas_call(
        kernel,
        out_shape=jax.ShapeDtypeStruct((piece, width), half),
        in_specs=[pl.BlockSpec(memory_space=pl.ANY)] * 5,
        out_specs=pl.BlockSpec(memory_space=pltpu.VMEM),
        scratch_shapes=scratch,
        compiler_params=pltpu.CompilerParams(
            collective_id=0, has_side_effects=True, vmem_limit_bytes=60 * 1024 * 1024
        ),
    )(
        queries, key_vectors.reshape(grid), value_vectors.reshape(grid), out_weight, window
    )


def solution(mesh):
    in_specs = (
        P(("batch", "seq"), "head"),
        P(("batch", "seq"), "head"),
        P(("batch", "seq"), "head"),
        P("head", None),
        P(("batch", "seq"), None),
    )
    out_specs = P(("batch", "seq", "head"), None)
    return jax.shard_map(
        per_device, mesh=mesh, in_specs=in_specs, out_specs=out_specs, check_vma=False
    )
```

```python
import functools

import jax
import jax.numpy as jnp
from jax import lax
from jax.experimental import pallas as pl
from jax.experimental.pallas import tpu as pltpu
from jax.sharding import PartitionSpec as P

DH = 128
HPD = 3
ROW = 4
COLUMNS = 4
WINDOW = 3
RING = 4
HEAD_DEVICES = 8
PIECES = 2
GATE = (0, 0)
SLOTS = 5
MESH = pl.DeviceIdType.MESH


def keys_of(ref, window, column, step):
    slot = lax.rem(window[0, column] + step, SLOTS)
    rows = ref[slot, pl.ds(window[1, column], WINDOW)]
    return rows.reshape(rows.shape[0] * rows.shape[1], DH)


def scores_of(q, ref, window, column, step):
    return lax.dot_general(
        q,
        keys_of(ref, window, column, step),
        (((1,), (1,)), ((), ())),
        preferred_element_type=jnp.float32,
    )


def lane_sums(powers):
    part = powers[:, :DH]
    for lane in range(DH, powers.shape[1], DH):
        part = part + powers[:, lane : lane + DH]
    return part


def attend(q_ref, k_ref, v_ref, o_ref, window, column, tile, factor):
    rows = pl.ds(pl.multiple_of(column * tile, tile), tile)
    q = q_ref[rows, :]
    top = None
    for step in range(WINDOW):
        scores = scores_of(q, k_ref, window, column, step)
        highest = jnp.max(scores, axis=-1, keepdims=True)
        if top is not None:
            highest = jnp.maximum(top, highest)
        powers = jnp.exp2((scores - highest) * factor)
        part = lane_sums(powers)
        mixed = jnp.dot(
            powers.astype(jnp.bfloat16),
            keys_of(v_ref, window, column, step),
            preferred_element_type=jnp.float32,
        )
        if top is None:
            total, acc = part, mixed
        else:
            fade = jnp.exp2((top - highest) * factor)
            total, acc = total * fade + part, acc * fade + mixed
        top = highest
    total = jnp.sum(total, axis=-1, keepdims=True)
    o_ref[rows, :] = (acc / total).astype(jnp.bfloat16)


def weigh(q_ref, k_ref, weights, totals, window, column, tile, factor):
    rows = pl.ds(pl.multiple_of(column * tile, tile), tile)
    q = q_ref[rows, :]
    scores = [scores_of(q, k_ref, window, column, step) for step in range(WINDOW)]
    highest = functools.reduce(
        jnp.maximum, [jnp.max(term, axis=-1, keepdims=True) for term in scores]
    )
    total = None
    for step in range(WINDOW):
        powers = jnp.exp2((scores[step] - highest) * factor)
        part = lane_sums(powers)
        total = part if total is None else total + part
        weights[column, step] = powers.astype(jnp.bfloat16)
    totals[rows, :] = total


def mix(v_ref, o_ref, weights, totals, window, column, tile):
    rows = pl.ds(pl.multiple_of(column * tile, tile), tile)
    acc = None
    for step in range(WINDOW):
        mixed = jnp.dot(
            weights[column, step],
            keys_of(v_ref, window, column, step),
            preferred_element_type=jnp.float32,
        )
        acc = mixed if acc is None else acc + mixed
    total = jnp.sum(totals[rows, :], axis=-1, keepdims=True)
    o_ref[rows, :] = (acc / total).astype(jnp.bfloat16)


def kernel(
    q_hbm, k_hbm, v_hbm, w_hbm, win_hbm, out_ref,
    k0, k1, k2, v0, v1, v2, q0, q1, q2, o0, o1, o2, a0, a1, a2, w0, w1, w2,
    acc, weights, totals, window,
    kv_recv, kv_send, q_recv, q_send, win_recv, win_send,
    w_own, w_recv, w_send, a_recv, a_send, row_open,
):
    ks, vs, qs, os_, as_, ws = (
        (k0, k1, k2), (v0, v1, v2), (q0, q1, q2), (o0, o1, o2), (a0, a1, a2), (w0, w1, w2),
    )
    kv = (ks, vs)
    kv_hbm = (k_hbm, v_hbm)
    tokens = q_hbm.shape[0]
    tile = tokens // COLUMNS
    piece = tokens // HEAD_DEVICES
    width = w_hbm.shape[1]
    factor = DH ** (-0.5) * 1.4426950408889634

    b = lax.axis_index("batch")
    s = lax.axis_index("seq")
    h = lax.axis_index("head")
    y, zh = s // ROW, s % ROW
    x, c = h // 2, h % 2
    g = zh // 2
    near = c == g
    far = c != g
    u = zh + g * (3 - 2 * zh)
    f = 1 - 2 * c
    spin = f * (1 - 2 * u)
    other = 2 * x + 1 - c
    zq = jnp.where(near, zh, 3 - zh)
    sq = ROW * y + zq
    hq = 2 * x + g
    y_next = (y - f + ROW) % ROW
    z_dev = (b, ROW * y + zh + 1 - 2 * (zh % 2), h)
    sib = (b, s, other)
    y_dev = (b, ROW * y_next + zh, other)
    b_dev = (b, jnp.where(u == 0, ROW * y_next + zh, s), other)
    partner_seq = ROW * y + 3 - zh
    partner = (b, partner_seq, other)
    xp, xm, xo = (x + 1) % RING, (x + 3) % RING, (x + 2) % RING
    xp_dev, xm_dev = (b, s, 2 * xp + c), (b, s, 2 * xm + c)

    def remote(src, dst, send, recv, device):
        return pltpu.make_async_remote_copy(
            src_ref=src, dst_ref=dst, send_sem=send, recv_sem=recv,
            device_id=device, device_id_type=MESH,
        )

    barrier = pltpu.get_barrier_semaphore()
    for device in (z_dev, y_dev, sib, xp_dev, xm_dev):
        pl.semaphore_signal(barrier, inc=1, device_id=device, device_id_type=MESH)

    @pl.when(far)
    def _():
        pl.semaphore_signal(barrier, inc=1, device_id=partner, device_id_type=MESH)

    pl.semaphore_wait(barrier, jnp.where(far, 6, 5))
    for device in (sib, xp_dev, xm_dev):
        pl.semaphore_signal(row_open.at[0], inc=1, device_id=device, device_id_type=MESH)

    def slot_of(first, offset):
        return (first + offset + SLOTS) % SLOTS

    own = slot_of(sq, 0)
    given = slot_of(s, 0)
    crossed = slot_of(sq, spin)
    y_first = ROW * y_next + 3 - zq

    def head_columns(n):
        return pl.ds(n * DH, DH)

    def part(p):
        count = COLUMNS // PIECES
        return pl.ds(p * count, count)

    def give(n, which, p):
        return remote(
            kv_hbm[which].at[part(p), :, head_columns(n)], kv[which][n].at[given, part(p)],
            kv_send.at[n, which, 0, p], kv_recv.at[n, which, given, p], partner,
        )

    def keep(n, which, p):
        return pltpu.make_async_copy(
            kv_hbm[which].at[part(p), :, head_columns(n)],
            kv[which][n].at[own, part(p)],
            kv_recv.at[n, which, own, p],
        )

    def give_q(n):
        return remote(q_hbm.at[:, head_columns(n)], qs[n], q_send.at[n], q_recv.at[n], partner)

    def keep_q(n):
        return pltpu.make_async_copy(q_hbm.at[:, head_columns(n)], qs[n], q_recv.at[n])

    give_win = remote(win_hbm, window, win_send, win_recv, partner)
    keep_win = pltpu.make_async_copy(win_hbm, window, win_recv)

    def relay(n, which, number, p):
        src, dst, device = (
            (own, own, z_dev),
            (own, jnp.where(u == 0, slot_of(y_first, f), own), b_dev),
            (crossed, crossed, sib),
            (crossed, slot_of(y_first, 2 * f), y_dev),
        )[number]
        buf = kv[which][n]
        return remote(
            buf.at[src, part(p)], buf.at[dst, part(p)],
            kv_send.at[n, which, number + 1, p], kv_recv.at[n, which, dst, p], device,
        )

    def landed(n, which, slot, p):
        pltpu.make_async_copy(
            kv_hbm[which].at[part(p), :, head_columns(n)],
            kv[which][n].at[slot, part(p)],
            kv_recv.at[n, which, slot, p],
        ).wait()

    def block(n, hd, first=0, count=DH):
        return ws[n].at[pl.ds(pl.multiple_of(hd * DH + first, 16), count), :]

    def own_rows(n):
        return w_hbm.at[pl.ds(n * DH, DH), :]

    half = DH // 2

    def w_copy(n, number):
        if number < 3:
            device = (xp_dev, xm_dev, sib)[number]
            recv = (0, 1, 4)[number]
            return remote(own_rows(n), block(n, h), w_send.at[n, number], w_recv.at[n, recv], device)
        if number == 3:
            part, recv, device = block(n, 2 * xm + c, 0, half), 2, xp_dev
        elif number == 4:
            part, recv, device = block(n, 2 * xp + c, half, half), 3, xm_dev
        else:
            part = block(n, 2 * (xm, xp, xo)[number - 5] + c)
            recv, device = number, sib
        return remote(part, part, w_send.at[n, number], w_recv.at[n, recv], device)

    def w_keep(n):
        return pltpu.make_async_copy(own_rows(n), block(n, h), w_own.at[n])

    def w_landed(n, recv):
        if recv < 2:
            part = block(n, 2 * (xm, xp)[recv] + c)
        elif recv == 2:
            part = block(n, 2 * xo + c, 0, half)
        elif recv == 3:
            part = block(n, 2 * xo + c, half, half)
        elif recv == 4:
            part = block(n, other)
        else:
            part = block(n, 2 * (xm, xp, xo)[recv - 5] + 1 - c)
        pltpu.make_async_copy(part, part, w_recv.at[n, recv]).wait()

    def w_second(n):
        w_landed(n, 0)
        w_copy(n, 3).start()
        w_copy(n, 5).start()
        w_landed(n, 1)
        w_copy(n, 4).start()
        w_copy(n, 6).start()

    def w_third(n):
        w_landed(n, 2)
        w_landed(n, 3)
        w_copy(n, 7).start()

    def w_all(n):
        for recv in range(4, 8):
            w_landed(n, recv)

    def first_relay(n, kinds=(0, 1)):
        for which in kinds:
            for p in range(PIECES):
                landed(n, which, own, p)
                relay(n, which, 0, p).start()
                relay(n, which, 1, p).start()

    def second_relay(n, which):
        for p in range(PIECES):
            landed(n, which, crossed, p)
            relay(n, which, 3, p).start()
            relay(n, which, 2, p).start()

    def o_rows(n, hd):
        return os_[n].at[pl.ds(pl.multiple_of(hd * piece, piece), piece), :]

    def o_place(n, head):
        return as_[n].at[:, pl.ds(pl.multiple_of(head * DH, DH), DH)]

    def o_copy(n, hd):
        return remote(
            o_rows(n, hd), o_place(n, hq), a_send.at[n, hd], a_recv.at[n, hq], (b, sq, hd)
        )

    def all_landed(n, which):
        for offset in (-spin, -2 * f):
            for p in range(PIECES):
                landed(n, which, slot_of(sq, offset), p)

        @pl.when(near if (n, which) == GATE else near | far)
        def _():
            for p in range(PIECES):
                landed(n, which, slot_of(sq, 2 * f), p)

    def send_rows(n, column):
        for core in range(2):
            hd = 2 * column + core
            mine = jnp.logical_and(near, hd == h)

            @pl.when(mine)
            def _():
                pltpu.make_async_copy(
                    o_rows(n, hd), o_place(n, hq), a_recv.at[n, hq]
                ).start()

            @pl.when(jnp.logical_not(mine))
            def _():
                o_copy(n, hd).start()

    def compute(n):
        all_landed(n, 0)
        all_landed(n, 1)
        keep_q(n).wait()

        @pl.loop(0, COLUMNS)
        def _(column):
            attend(qs[n], ks[n], vs[n], os_[n], window, column, tile, factor)
            send_rows(n, column)

    def compute_weights(n):
        all_landed(n, 0)
        keep_q(n).wait()

        @pl.loop(0, COLUMNS)
        def _(column):
            weigh(qs[n], ks[n], weights, totals, window, column, tile, factor)

    def compute_mix(n):
        all_landed(n, 1)

        @pl.loop(0, COLUMNS)
        def _(column):
            mix(vs[n], os_[n], weights, totals, window, column, tile)
            send_rows(n, column)

    chunk = 512

    def project(n):
        w_keep(n).wait()
        w_all(n)
        for hd in range(HEAD_DEVICES):
            pltpu.make_async_copy(
                o_rows(n, hd), o_place(n, hd), a_recv.at[n, hd]
            ).wait()

        @pl.loop(0, width // chunk)
        def _(j):
            columns = pl.ds(pl.multiple_of(j * chunk, chunk), chunk)
            term = jnp.dot(as_[n][...], ws[n][:, columns], preferred_element_type=jnp.float32)
            if n == 0:
                acc[:, columns] = term
            elif n < HPD - 1:
                acc[:, columns] += term
            else:
                out_ref[:, columns] = (acc[:, columns] + term).astype(jnp.bfloat16)

    @pl.when(near)
    def _():
        keep_win.start()
        for n in range(HPD):
            for which in range(2):
                for p in range(PIECES):
                    keep(n, which, p).start()
        for n in range(HPD):
            keep_q(n).start()

    @pl.when(far)
    def _():
        for n in range(HPD):
            for which in range(2):
                if n == HPD - 1 and which == 1:
                    give_q(n).start()
                for p in range(PIECES):
                    give(n, which, p).start()
            if n < HPD - 1:
                give_q(n).start()
            if n == 0:
                give_win.start()

    for n in range(HPD):
        w_keep(n).start()
        for number in range(3):
            w_copy(n, number).start()

    @pl.when(near)
    def _():
        first_relay(0)
        first_relay(1)
        first_relay(2)

    pl.semaphore_wait(row_open.at[0], 3)
    pl.semaphore_signal(row_open.at[1], inc=1, device_id=sib, device_id_type=MESH)
    w_second(0)
    @pl.when(near)
    def _():
        second_relay(0, 0)
        second_relay(0, 1)

    @pl.when(far)
    def _():
        for p in range(PIECES):
            landed(0, 0, slot_of(sq, 2 * f), p)
        first_relay(0)

    w_second(1)
    @pl.when(near)
    def _():
        second_relay(1, 0)
        second_relay(1, 1)

    @pl.when(far)
    def _():
        first_relay(1)
        second_relay(0, 0)
        second_relay(0, 1)

    pl.semaphore_wait(row_open.at[1], 1)

    @pl.when(far)
    def _():
        pl.semaphore_signal(row_open.at[2], inc=1, device_id=partner, device_id_type=MESH)

    keep_win.wait()

    @pl.when(far)
    def _():
        pl.semaphore_wait(row_open.at[2], 1)

    compute(0)
    w_second(2)
    @pl.when(near)
    def _():
        second_relay(2, 0)
        second_relay(2, 1)

    @pl.when(far)
    def _():
        first_relay(2, (0,))

    w_third(0)

    @pl.when(far)
    def _():
        second_relay(1, 0)
        second_relay(1, 1)
        first_relay(2, (1,))

    w_third(1)
    compute(1)
    w_third(2)
    @pl.when(far)
    def _():
        second_relay(2, 0)

    compute_weights(2)
    @pl.when(far)
    def _():
        second_relay(2, 1)

    compute_mix(2)
    project(0)
    project(1)
    project(2)

    for n in range(HPD):
        for which in range(2):
            for number in range(4):
                for p in range(PIECES):
                    relay(n, which, number, p).wait_send()
        for number in range(8):
            w_copy(n, number).wait_send()
        for hd in range(HEAD_DEVICES):

            @pl.when(jnp.logical_not(jnp.logical_and(near, hd == h)))
            def _():
                o_copy(n, hd).wait_send()

    @pl.when(far)
    def _():
        give_win.wait_send()
        for n in range(HPD):
            for which in range(2):
                for p in range(PIECES):
                    give(n, which, p).wait_send()
            give_q(n).wait_send()


def per_device(queries, key_vectors, value_vectors, out_weight, window_start):
    tokens = queries.shape[0]
    width = out_weight.shape[1]
    piece = tokens // HEAD_DEVICES
    half = jnp.bfloat16
    grid = (COLUMNS, tokens // COLUMNS, queries.shape[1])
    window = window_start.T
    dma = pltpu.SemaphoreType.DMA
    scratch = (
        [pltpu.VMEM((5, COLUMNS, tokens // COLUMNS, DH), half)] * 6
        + [pltpu.VMEM((tokens, DH), half)] * 6
        + [pltpu.VMEM((piece, HEAD_DEVICES * DH), half)] * 3
        + [pltpu.VMEM((HEAD_DEVICES * DH, width), half)] * 3
        + [
            pltpu.VMEM((piece, width), jnp.float32),
            pltpu.VMEM((COLUMNS, WINDOW, tokens // COLUMNS, WINDOW * tokens // COLUMNS), half),
            pltpu.VMEM((tokens, DH), jnp.float32),
            pltpu.SMEM(window.shape, jnp.int32),
            dma((HPD, 2, 5, PIECES)), dma((HPD, 2, 5, PIECES)), dma((HPD,)), dma((HPD,)), dma, dma,
            dma((HPD,)), dma((HPD, 8)), dma((HPD, 8)),
            dma((HPD, HEAD_DEVICES)), dma((HPD, HEAD_DEVICES)), pltpu.SemaphoreType.REGULAR((3,)),
        ]
    )
    return pl.pallas_call(
        kernel,
        out_shape=jax.ShapeDtypeStruct((piece, width), half),
        in_specs=[pl.BlockSpec(memory_space=pl.ANY)] * 5,
        out_specs=pl.BlockSpec(memory_space=pltpu.VMEM),
        scratch_shapes=scratch,
        compiler_params=pltpu.CompilerParams(
            collective_id=0, has_side_effects=True, vmem_limit_bytes=60 * 1024 * 1024
        ),
    )(
        queries, key_vectors.reshape(grid), value_vectors.reshape(grid), out_weight, window
    )


def solution(mesh):
    in_specs = (
        P(("batch", "seq"), "head"),
        P(("batch", "seq"), "head"),
        P(("batch", "seq"), "head"),
        P("head", None),
        P(("batch", "seq"), None),
    )
    out_specs = P(("batch", "seq", "head"), None)
    return jax.shard_map(
        per_device, mesh=mesh, in_specs=in_specs, out_specs=out_specs, check_vma=False
    )
```

```python
import functools

import jax
import jax.numpy as jnp
from jax import lax
from jax.experimental import pallas as pl
from jax.experimental.pallas import tpu as pltpu
from jax.sharding import PartitionSpec as P

DH = 128
HPD = 3
ROW = 4
COLUMNS = 4
WINDOW = 3
RING = 4
HEAD_DEVICES = 8
PIECES = 2
GATE = (0, 0)
SLOTS = 5
MESH = pl.DeviceIdType.MESH


def keys_of(ref, window, column, step):
    slot = lax.rem(window[0, column] + step, SLOTS)
    rows = ref[slot, pl.ds(window[1, column], WINDOW)]
    return rows.reshape(rows.shape[0] * rows.shape[1], DH)


def scores_of(q, ref, window, column, step):
    return lax.dot_general(
        q,
        keys_of(ref, window, column, step),
        (((1,), (1,)), ((), ())),
        preferred_element_type=jnp.float32,
    )


def lane_sums(powers):
    part = powers[:, :DH]
    for lane in range(DH, powers.shape[1], DH):
        part = part + powers[:, lane : lane + DH]
    return part


def attend(q_ref, k_ref, v_ref, o_ref, window, column, tile, factor):
    rows = pl.ds(pl.multiple_of(column * tile, tile), tile)
    q = q_ref[rows, :]
    top = None
    for step in range(WINDOW):
        scores = scores_of(q, k_ref, window, column, step)
        highest = jnp.max(scores, axis=-1, keepdims=True)
        if top is not None:
            highest = jnp.maximum(top, highest)
        powers = jnp.exp2((scores - highest) * factor)
        part = lane_sums(powers)
        mixed = jnp.dot(
            powers.astype(jnp.bfloat16),
            keys_of(v_ref, window, column, step),
            preferred_element_type=jnp.float32,
        )
        if top is None:
            total, acc = part, mixed
        else:
            fade = jnp.exp2((top - highest) * factor)
            total, acc = total * fade + part, acc * fade + mixed
        top = highest
    total = jnp.sum(total, axis=-1, keepdims=True)
    o_ref[rows, :] = (acc / total).astype(jnp.bfloat16)


def weigh(q_ref, k_ref, weights, totals, window, column, tile, factor):
    rows = pl.ds(pl.multiple_of(column * tile, tile), tile)
    q = q_ref[rows, :]
    scores = [scores_of(q, k_ref, window, column, step) for step in range(WINDOW)]
    highest = functools.reduce(
        jnp.maximum, [jnp.max(term, axis=-1, keepdims=True) for term in scores]
    )
    total = None
    for step in range(WINDOW):
        powers = jnp.exp2((scores[step] - highest) * factor)
        part = lane_sums(powers)
        total = part if total is None else total + part
        weights[column, step] = powers.astype(jnp.bfloat16)
    totals[rows, :] = total


def mix(v_ref, o_ref, weights, totals, window, column, tile):
    rows = pl.ds(pl.multiple_of(column * tile, tile), tile)
    acc = None
    for step in range(WINDOW):
        mixed = jnp.dot(
            weights[column, step],
            keys_of(v_ref, window, column, step),
            preferred_element_type=jnp.float32,
        )
        acc = mixed if acc is None else acc + mixed
    total = jnp.sum(totals[rows, :], axis=-1, keepdims=True)
    o_ref[rows, :] = (acc / total).astype(jnp.bfloat16)


def kernel(
    q_hbm, k_hbm, v_hbm, w_hbm, win_hbm, out_ref,
    k0, k1, k2, v0, v1, v2, q0, q1, q2, o0, o1, o2, a0, a1, a2, w0, w1, w2,
    acc, weights, totals, window,
    kv_recv, kv_send, q_recv, q_send, win_recv, win_send,
    w_own, w_recv, w_send, a_recv, a_send, row_open,
):
    ks, vs, qs, os_, as_, ws = (
        (k0, k1, k2), (v0, v1, v2), (q0, q1, q2), (o0, o1, o2), (a0, a1, a2), (w0, w1, w2),
    )
    kv = (ks, vs)
    kv_hbm = (k_hbm, v_hbm)
    tokens = q_hbm.shape[0]
    tile = tokens // COLUMNS
    piece = tokens // HEAD_DEVICES
    width = w_hbm.shape[1]
    factor = DH ** (-0.5) * 1.4426950408889634

    b = lax.axis_index("batch")
    s = lax.axis_index("seq")
    h = lax.axis_index("head")
    y, zh = s // ROW, s % ROW
    x, c = h // 2, h % 2
    g = zh // 2
    near = c == g
    far = c != g
    u = zh + g * (3 - 2 * zh)
    f = 1 - 2 * c
    spin = f * (1 - 2 * u)
    other = 2 * x + 1 - c
    zq = jnp.where(near, zh, 3 - zh)
    sq = ROW * y + zq
    hq = 2 * x + g
    y_next = (y - f + ROW) % ROW
    z_dev = (b, ROW * y + zh + 1 - 2 * (zh % 2), h)
    sib = (b, s, other)
    y_dev = (b, ROW * y_next + zh, other)
    b_dev = (b, jnp.where(u == 0, ROW * y_next + zh, s), other)
    partner_seq = ROW * y + 3 - zh
    partner = (b, partner_seq, other)
    xp, xm, xo = (x + 1) % RING, (x + 3) % RING, (x + 2) % RING
    xp_dev, xm_dev = (b, s, 2 * xp + c), (b, s, 2 * xm + c)

    def remote(src, dst, send, recv, device):
        return pltpu.make_async_remote_copy(
            src_ref=src, dst_ref=dst, send_sem=send, recv_sem=recv,
            device_id=device, device_id_type=MESH,
        )

    barrier = pltpu.get_barrier_semaphore()
    for device in (z_dev, y_dev, sib, xp_dev, xm_dev):
        pl.semaphore_signal(barrier, inc=1, device_id=device, device_id_type=MESH)

    @pl.when(far)
    def _():
        pl.semaphore_signal(barrier, inc=1, device_id=partner, device_id_type=MESH)

    pl.semaphore_wait(barrier, jnp.where(far, 6, 5))
    for device in (sib, xp_dev, xm_dev):
        pl.semaphore_signal(row_open.at[0], inc=1, device_id=device, device_id_type=MESH)

    def slot_of(first, offset):
        return (first + offset + SLOTS) % SLOTS

    own = slot_of(sq, 0)
    given = slot_of(s, 0)
    crossed = slot_of(sq, spin)
    y_first = ROW * y_next + 3 - zq

    def head_columns(n):
        return pl.ds(n * DH, DH)

    def part(p):
        count = COLUMNS // PIECES
        return pl.ds(p * count, count)

    def give(n, which, p):
        return remote(
            kv_hbm[which].at[part(p), :, head_columns(n)], kv[which][n].at[given, part(p)],
            kv_send.at[n, which, 0, p], kv_recv.at[n, which, given, p], partner,
        )

    def keep(n, which, p):
        return pltpu.make_async_copy(
            kv_hbm[which].at[part(p), :, head_columns(n)],
            kv[which][n].at[own, part(p)],
            kv_recv.at[n, which, own, p],
        )

    def give_q(n):
        return remote(q_hbm.at[:, head_columns(n)], qs[n], q_send.at[n], q_recv.at[n], partner)

    def keep_q(n):
        return pltpu.make_async_copy(q_hbm.at[:, head_columns(n)], qs[n], q_recv.at[n])

    give_win = remote(win_hbm, window, win_send, win_recv, partner)
    keep_win = pltpu.make_async_copy(win_hbm, window, win_recv)

    def relay(n, which, number, p):
        src, dst, device = (
            (own, own, z_dev),
            (own, jnp.where(u == 0, slot_of(y_first, f), own), b_dev),
            (crossed, crossed, sib),
            (crossed, slot_of(y_first, 2 * f), y_dev),
        )[number]
        buf = kv[which][n]
        return remote(
            buf.at[src, part(p)], buf.at[dst, part(p)],
            kv_send.at[n, which, number + 1, p], kv_recv.at[n, which, dst, p], device,
        )

    def landed(n, which, slot, p):
        pltpu.make_async_copy(
            kv_hbm[which].at[part(p), :, head_columns(n)],
            kv[which][n].at[slot, part(p)],
            kv_recv.at[n, which, slot, p],
        ).wait()

    def block(n, hd, first=0, count=DH):
        return ws[n].at[pl.ds(pl.multiple_of(hd * DH + first, 16), count), :]

    def own_rows(n):
        return w_hbm.at[pl.ds(n * DH, DH), :]

    half = DH // 2

    def w_copy(n, number):
        if number < 3:
            device = (xp_dev, xm_dev, sib)[number]
            recv = (0, 1, 4)[number]
            return remote(own_rows(n), block(n, h), w_send.at[n, number], w_recv.at[n, recv], device)
        if number == 3:
            part, recv, device = block(n, 2 * xm + c, 0, half), 2, xp_dev
        elif number == 4:
            part, recv, device = block(n, 2 * xp + c, half, half), 3, xm_dev
        else:
            part = block(n, 2 * (xm, xp, xo)[number - 5] + c)
            recv, device = number, sib
        return remote(part, part, w_send.at[n, number], w_recv.at[n, recv], device)

    def w_keep(n):
        return pltpu.make_async_copy(own_rows(n), block(n, h), w_own.at[n])

    def w_landed(n, recv):
        if recv < 2:
            part = block(n, 2 * (xm, xp)[recv] + c)
        elif recv == 2:
            part = block(n, 2 * xo + c, 0, half)
        elif recv == 3:
            part = block(n, 2 * xo + c, half, half)
        elif recv == 4:
            part = block(n, other)
        else:
            part = block(n, 2 * (xm, xp, xo)[recv - 5] + 1 - c)
        pltpu.make_async_copy(part, part, w_recv.at[n, recv]).wait()

    def w_second(n):
        w_landed(n, 0)
        w_copy(n, 3).start()
        w_copy(n, 5).start()
        w_landed(n, 1)
        w_copy(n, 4).start()
        w_copy(n, 6).start()

    def w_third(n):
        w_landed(n, 2)
        w_landed(n, 3)
        w_copy(n, 7).start()

    def w_all(n):
        for recv in range(4, 8):
            w_landed(n, recv)

    def first_relay(n, kinds=(0, 1)):
        for which in kinds:
            for p in range(PIECES):
                landed(n, which, own, p)
                relay(n, which, 0, p).start()
                relay(n, which, 1, p).start()

    def second_piece(n, which, p):
        landed(n, which, crossed, p)
        relay(n, which, 3, p).start()
        relay(n, which, 2, p).start()

    def second_relay(n, which):
        for p in range(PIECES):
            second_piece(n, which, p)

    def o_rows(n, hd):
        return os_[n].at[pl.ds(pl.multiple_of(hd * piece, piece), piece), :]

    def o_place(n, head):
        return as_[n].at[:, pl.ds(pl.multiple_of(head * DH, DH), DH)]

    def o_copy(n, hd):
        return remote(
            o_rows(n, hd), o_place(n, hq), a_send.at[n, hd], a_recv.at[n, hq], (b, sq, hd)
        )

    def all_landed(n, which):
        for offset in (-spin, -2 * f):
            for p in range(PIECES):
                landed(n, which, slot_of(sq, offset), p)

        @pl.when(near if (n, which) == GATE else near | far)
        def _():
            for p in range(PIECES):
                landed(n, which, slot_of(sq, 2 * f), p)

    def send_rows(n, column):
        for core in range(2):
            hd = 2 * column + core
            mine = jnp.logical_and(near, hd == h)

            @pl.when(mine)
            def _():
                pltpu.make_async_copy(
                    o_rows(n, hd), o_place(n, hq), a_recv.at[n, hq]
                ).start()

            @pl.when(jnp.logical_not(mine))
            def _():
                o_copy(n, hd).start()

    def compute(n):
        all_landed(n, 0)
        all_landed(n, 1)
        keep_q(n).wait()

        @pl.loop(0, COLUMNS)
        def _(column):
            attend(qs[n], ks[n], vs[n], os_[n], window, column, tile, factor)
            send_rows(n, column)

    def compute_weights(n):
        all_landed(n, 0)
        keep_q(n).wait()

        @pl.loop(0, COLUMNS)
        def _(column):
            for p in range(PIECES):

                @pl.when(jnp.logical_and(far, column == COLUMNS - PIECES + p))
                def _():
                    second_piece(n, 1, p)

            weigh(qs[n], ks[n], weights, totals, window, column, tile, factor)

    def compute_mix(n):
        all_landed(n, 1)

        @pl.loop(0, COLUMNS)
        def _(column):
            mix(vs[n], os_[n], weights, totals, window, column, tile)
            send_rows(n, column)

    chunk = 512

    def project(n):
        w_keep(n).wait()
        w_all(n)
        for hd in range(HEAD_DEVICES):
            pltpu.make_async_copy(
                o_rows(n, hd), o_place(n, hd), a_recv.at[n, hd]
            ).wait()

        @pl.loop(0, width // chunk)
        def _(j):
            columns = pl.ds(pl.multiple_of(j * chunk, chunk), chunk)
            term = jnp.dot(as_[n][...], ws[n][:, columns], preferred_element_type=jnp.float32)
            if n == 0:
                acc[:, columns] = term
            elif n < HPD - 1:
                acc[:, columns] += term
            else:
                out_ref[:, columns] = (acc[:, columns] + term).astype(jnp.bfloat16)

    @pl.when(near)
    def _():
        keep_win.start()
        for n in range(HPD):
            for which in range(2):
                for p in range(PIECES):
                    keep(n, which, p).start()
        for n in range(HPD):
            keep_q(n).start()

    @pl.when(far)
    def _():
        for n in range(HPD):
            for which in range(2):
                if n == HPD - 1 and which == 1:
                    give_q(n).start()
                for p in range(PIECES):
                    give(n, which, p).start()
            if n < HPD - 1:
                give_q(n).start()
            if n == 0:
                give_win.start()

    for n in range(HPD):
        w_keep(n).start()
        for number in range(3):
            w_copy(n, number).start()

    @pl.when(near)
    def _():
        first_relay(0)
        first_relay(1)
        first_relay(2)

    pl.semaphore_wait(row_open.at[0], 3)
    pl.semaphore_signal(row_open.at[1], inc=1, device_id=sib, device_id_type=MESH)
    w_second(0)
    @pl.when(near)
    def _():
        second_relay(0, 0)
        second_relay(0, 1)

    @pl.when(far)
    def _():
        for p in range(PIECES):
            landed(0, 0, slot_of(sq, 2 * f), p)
        first_relay(0)

    w_second(1)
    @pl.when(near)
    def _():
        second_relay(1, 0)
        second_relay(1, 1)

    @pl.when(far)
    def _():
        first_relay(1)
        second_relay(0, 0)
        second_relay(0, 1)

    pl.semaphore_wait(row_open.at[1], 1)

    @pl.when(far)
    def _():
        pl.semaphore_signal(row_open.at[2], inc=1, device_id=partner, device_id_type=MESH)

    keep_win.wait()

    @pl.when(far)
    def _():
        pl.semaphore_wait(row_open.at[2], 1)

    compute(0)
    w_second(2)
    @pl.when(near)
    def _():
        second_relay(2, 0)
        second_relay(2, 1)

    @pl.when(far)
    def _():
        first_relay(2, (0,))

    w_third(0)

    @pl.when(far)
    def _():
        second_relay(1, 0)
        second_relay(1, 1)
        first_relay(2, (1,))

    w_third(1)
    compute(1)
    w_third(2)
    @pl.when(far)
    def _():
        second_relay(2, 0)

    compute_weights(2)
    compute_mix(2)
    project(0)
    project(1)
    project(2)

    for n in range(HPD):
        for which in range(2):
            for number in range(4):
                for p in range(PIECES):
                    relay(n, which, number, p).wait_send()
        for number in range(8):
            w_copy(n, number).wait_send()
        for hd in range(HEAD_DEVICES):

            @pl.when(jnp.logical_not(jnp.logical_and(near, hd == h)))
            def _():
                o_copy(n, hd).wait_send()

    @pl.when(far)
    def _():
        give_win.wait_send()
        for n in range(HPD):
            for which in range(2):
                for p in range(PIECES):
                    give(n, which, p).wait_send()
            give_q(n).wait_send()


def per_device(queries, key_vectors, value_vectors, out_weight, window_start):
    tokens = queries.shape[0]
    width = out_weight.shape[1]
    piece = tokens // HEAD_DEVICES
    half = jnp.bfloat16
    grid = (COLUMNS, tokens // COLUMNS, queries.shape[1])
    window = window_start.T
    dma = pltpu.SemaphoreType.DMA
    scratch = (
        [pltpu.VMEM((5, COLUMNS, tokens // COLUMNS, DH), half)] * 6
        + [pltpu.VMEM((tokens, DH), half)] * 6
        + [pltpu.VMEM((piece, HEAD_DEVICES * DH), half)] * 3
        + [pltpu.VMEM((HEAD_DEVICES * DH, width), half)] * 3
        + [
            pltpu.VMEM((piece, width), jnp.float32),
            pltpu.VMEM((COLUMNS, WINDOW, tokens // COLUMNS, WINDOW * tokens // COLUMNS), half),
            pltpu.VMEM((tokens, DH), jnp.float32),
            pltpu.SMEM(window.shape, jnp.int32),
            dma((HPD, 2, 5, PIECES)), dma((HPD, 2, 5, PIECES)), dma((HPD,)), dma((HPD,)), dma, dma,
            dma((HPD,)), dma((HPD, 8)), dma((HPD, 8)),
            dma((HPD, HEAD_DEVICES)), dma((HPD, HEAD_DEVICES)), pltpu.SemaphoreType.REGULAR((3,)),
        ]
    )
    return pl.pallas_call(
        kernel,
        out_shape=jax.ShapeDtypeStruct((piece, width), half),
        in_specs=[pl.BlockSpec(memory_space=pl.ANY)] * 5,
        out_specs=pl.BlockSpec(memory_space=pltpu.VMEM),
        scratch_shapes=scratch,
        compiler_params=pltpu.CompilerParams(
            collective_id=0, has_side_effects=True, vmem_limit_bytes=60 * 1024 * 1024
        ),
    )(
        queries, key_vectors.reshape(grid), value_vectors.reshape(grid), out_weight, window
    )


def solution(mesh):
    in_specs = (
        P(("batch", "seq"), "head"),
        P(("batch", "seq"), "head"),
        P(("batch", "seq"), "head"),
        P("head", None),
        P(("batch", "seq"), None),
    )
    out_specs = P(("batch", "seq", "head"), None)
    return jax.shard_map(
        per_device, mesh=mesh, in_specs=in_specs, out_specs=out_specs, check_vma=False
    )
```
